32 devices in a mesh: dev: 8 (over y, x, core), rep: 4 (over z).
Axes of the slice: x: 2, y: 2, z: 4, core: 2. Of those that a mesh axis runs over, the one named last changes fastest.
Arguments:
- backbone: bfloat16 [32, 16, 8, 512], P(('rep', 'dev')), parts along dimension 0, may hold values from -6 to 6
- conv_weight: bfloat16 [3, 3, 512, 2048], P(None, None, None, ('rep', 'dev')), parts along dimension 3, may hold values from -0.35355339 to 0.35355339
- smooth_weight: float32 [3, 3, 2048], P(None, None, 'rep'), parts along dimension 2, may hold values from -2.5 to 2.5
Outputs:
- smoothed: bfloat16 [32, 16, 8, 512], P(('rep', 'dev')), parts along dimension 0
The draws below stay inside these ranges and needn't reach their ends.
There are 4 independent parts, one for each index of `rep`. The reference program is written for one: setup_inputs(seed, part) draws one part's arguments, and reference() takes and returns one part's arrays. A program takes and returns all parts, laid end to end along the dimension named above; each array names one. Nothing has to cross between parts.
All inputs are finite; a program needn't handle non-finite values.
Results may differ from the reference program's by a relative error of at most 0.0073.
Values may be sent and summed in bfloat16 or wider, within the bound.
A program may use at most 64 MiB of HBM per device.

```python
import jax
import jax.numpy as jnp
from jax import lax

C = 512
GRID_H = 16
GRID_W = 8
ITERS = 2
IMAGES = 8


def draw_conv_weight(key, part):
    base_key = jax.random.fold_in(key, 11)
    scale_key = jax.random.fold_in(key, 23)
    base = jnp.clip(jax.random.normal(base_key, (3, 3, C, C), jnp.float32), -6.0, 6.0)
    scales = jnp.exp(jax.random.uniform(scale_key, (C,), jnp.float32, jnp.log(0.3), jnp.log(3.0)))
    weights = base * scales / jnp.sqrt(9.0 * C)
    return weights.astype(jnp.bfloat16)


def block_levels(rng, dims, split, least, largest):
    gain = 1.0
    for axis_at, parts in split:
        steps = jax.random.uniform(jax.random.fold_in(jax.random.fold_in(rng, 6), axis_at), (parts,), jnp.float32, least / len(split), largest / len(split))
        gain = gain * jnp.repeat(jnp.exp(steps), dims[axis_at] // parts).reshape((-1,) + (1,) * (len(dims) - 1 - axis_at))
    return gain


def bell_draw(stream_key, shape, deviation, reach, split=(), kind=jnp.bfloat16):
    factor_of = block_levels(stream_key, shape, split, -0.22, 0.18) if split else 1.0
    values = jax.random.normal(stream_key, shape, jnp.float32) * deviation * factor_of
    return jnp.minimum(jnp.maximum(values, -reach), reach).astype(kind)


def setup_inputs(seed: int = 0, part: int = 0) -> dict:
    key_of = jax.random.split(jax.random.key(seed), 4)
    part_keys = jax.random.split(jax.random.fold_in(key_of[3], part), 4)
    return {
        "backbone": bell_draw(part_keys[0], (IMAGES, GRID_H, GRID_W, C), 1.0, 6.0, ((0, 8),)),
        "conv_weight": draw_conv_weight(jax.random.fold_in(jax.random.fold_in(key_of[3], part), 71), part),
        "smooth_weight": bell_draw(part_keys[2], (3, 3, C), 0.35, 2.5, (), jnp.float32),
    }


ridge_term = 0.5

def convolve(padded, weights, grid_rows, grid_cols):
    summed = None
    for row_tap in range(3):
        for col_tap in range(3):
            window = padded[:, row_tap:row_tap + grid_rows, col_tap:col_tap + grid_cols, :]
            flat_window = window.reshape(-1, window.shape[3])
            product = jnp.dot(flat_window, weights[row_tap, col_tap], preferred_element_type=jnp.float32)
            summed = product if summed is None else summed + product
    return summed.reshape(padded.shape[0], grid_rows, grid_cols, weights.shape[3])

def newton_root(moments):
    identity = jnp.eye(C, dtype=jnp.float32)
    frob = jnp.sqrt(jnp.sum(moments * moments))
    upper = moments / frob
    lower = identity
    for sweep in range(ITERS):
        product = jnp.dot(lower, upper, precision=lax.Precision.HIGHEST)
        factor = 1.5 * identity - 0.5 * product
        if sweep + 1 < ITERS:
            upper = jnp.dot(upper, factor, precision=lax.Precision.HIGHEST)
        lower = jnp.dot(factor, lower, precision=lax.Precision.HIGHEST)
    return lower / jnp.sqrt(frob)

def reference(backbone, conv_weight, smooth_weight):
    image_count = backbone.shape[0]
    padded = jnp.pad(backbone, ((0, 0), (1, 1), (1, 1), (0, 0)))
    features = convolve(padded, conv_weight, GRID_H, GRID_W).astype(jnp.bfloat16)
    columns = features.reshape(image_count, GRID_H * GRID_W, C).transpose(1, 0, 2)
    identity = jnp.eye(C, dtype=jnp.float32)

    def per_position(column):
        center = lax.optimization_barrier(jnp.sum(column.astype(jnp.float32), axis=0)) / image_count
        centered = (column.astype(jnp.float32) - center).astype(jnp.bfloat16)
        gram = jnp.dot(centered.T, centered, preferred_element_type=jnp.float32)
        moments = gram / (image_count - 1) + ridge_term * identity
        inverse_root = newton_root(moments).astype(jnp.bfloat16)
        return jnp.dot(centered, inverse_root, preferred_element_type=jnp.float32).astype(jnp.bfloat16)
    whitened = lax.map(per_position, columns)
    whitened = whitened.transpose(1, 0, 2).reshape(image_count, GRID_H, GRID_W, C)
    padded_white = jnp.pad(whitened, ((0, 0), (1, 1), (1, 1), (0, 0)))
    summed = jnp.zeros((image_count, GRID_H, GRID_W, C), jnp.float32)
    for row_tap in range(3):
        for col_tap in range(3):
            window = padded_white[:, row_tap:row_tap + GRID_H, col_tap:col_tap + GRID_W, :]
            summed = summed + window.astype(jnp.float32) * smooth_weight[row_tap, col_tap]
    return summed.astype(jnp.bfloat16)
```

```python
import functools

import jax
import jax.numpy as jnp
from jax import lax
from jax.experimental import pallas as pl
from jax.experimental.pallas import tpu as pltpu
from jax.sharding import PartitionSpec as P

ITERS = 2
MESH = pl.DeviceIdType.MESH


ridge_term = 0.5


def convolve(padded, weights, grid_rows, grid_cols):
    summed = None
    for row_tap in range(3):
        for col_tap in range(3):
            window = padded[:, row_tap : row_tap + grid_rows, col_tap : col_tap + grid_cols, :]
            flat_window = window.reshape(-1, window.shape[3])
            product = jnp.dot(
                flat_window, weights[row_tap, col_tap], preferred_element_type=jnp.float32
            )
            summed = product if summed is None else summed + product
    return summed.reshape(padded.shape[0], grid_rows, grid_cols, weights.shape[3])


def single_root(moments):
    identity = jnp.eye(moments.shape[0], dtype=jnp.float32)
    frob = jnp.sqrt(jnp.sum(moments * moments))
    upper = moments / frob
    lower = identity
    for sweep in range(ITERS):
        product = jnp.dot(lower, upper, precision=lax.Precision.HIGHEST)
        factor = 1.5 * identity - 0.5 * product
        if sweep + 1 < ITERS:
            upper = jnp.dot(upper, factor, precision=lax.Precision.HIGHEST)
        lower = jnp.dot(factor, lower, precision=lax.Precision.HIGHEST)
    return lower / jnp.sqrt(frob)


def whiten_block(received):
    features_block = received[:, 0]
    image_count = features_block.shape[0]
    channels = features_block.shape[2]
    identity = jnp.eye(channels, dtype=jnp.float32)
    center = jnp.sum(features_block.astype(jnp.float32), axis=0) / image_count
    centered = (features_block.astype(jnp.float32) - center).astype(jnp.bfloat16)
    gram = jnp.einsum("nkc,nkd->kcd", centered, centered, preferred_element_type=jnp.float32)
    moments = gram / (image_count - 1) + ridge_term * identity
    roots = lax.map(single_root, moments)
    roots = roots.astype(jnp.bfloat16)
    whitened = jnp.einsum(
        "nkc,kcd->nkd", centered, roots, preferred_element_type=jnp.float32
    ).astype(jnp.bfloat16)
    return whitened[:, None]


def shards(backbone, conv_weight, smooth_weight):
    local_images = backbone.shape[0]
    grid_rows = backbone.shape[1]
    grid_cols = backbone.shape[2]
    channels = backbone.shape[3]
    owners = lax.axis_size("dev")
    padded = jnp.pad(backbone, ((0, 0), (1, 1), (1, 1), (0, 0)))
    kernel = lax.all_gather(conv_weight, "dev", axis=3, tiled=True)
    conv_out = convolve(padded, kernel, grid_rows, grid_cols)
    per_owner = grid_rows * grid_cols // owners
    features = conv_out.astype(jnp.bfloat16).reshape(local_images, owners, per_owner, channels)
    whitened = whiten_block(
        lax.all_to_all(features, "dev", split_axis=1, concat_axis=0, tiled=True)
    )
    returned = lax.all_to_all(whitened, "dev", split_axis=0, concat_axis=1, tiled=True)
    returned = returned.reshape(local_images, grid_rows, grid_cols, channels)
    padded_white = jnp.pad(returned, ((0, 0), (1, 1), (1, 1), (0, 0)))
    summed = jnp.zeros((local_images, grid_rows, grid_cols, channels), jnp.float32)
    for row_tap in range(3):
        for col_tap in range(3):
            window = padded_white[
                :, row_tap : row_tap + grid_rows, col_tap : col_tap + grid_cols, :
            ]
            summed = summed + window.astype(jnp.float32) * smooth_weight[row_tap, col_tap]
    return summed.astype(jnp.bfloat16)


def flip(index, mask, bits):
    flipped = 0
    for bit in range(bits):
        digit = (index // 2**bit) % 2
        if (mask >> bit) & 1:
            digit = 1 - digit
        flipped = flipped + digit * 2**bit
    return flipped


def shift_lanes(values, step, keep):
    lanes = values.shape[-1]
    return jnp.where(keep, pltpu.roll(values, step % lanes, values.ndim - 1), 0.0)


def small_product(left, right):
    total = None
    for k in range(right.shape[0]):
        term = left[:, k : k + 1, :] * right[k : k + 1, :, :]
        total = term if total is None else total + term
    return total


def fused_kernel(
    grid_cols,
    images,
    channels,
    x_in,
    w_in,
    smooth_in,
    out_ref,
    x_all,
    w_own,
    smooth_wide,
    feats,
    k_all,
    mix,
    sent,
    local_sem,
    x_send,
    x_recv,
    k_send,
    k_recv,
    o_send,
    o_recv,
):
    bits = 3
    me = lax.axis_index("dev")
    positions = x_in.shape[0]
    own = feats.shape[1]
    half = positions // 2
    peers = [flip(me, mask, bits) for mask in range(images)]

    barrier = pltpu.get_barrier_semaphore()
    for mask in range(1, images):
        pl.semaphore_signal(
            barrier, inc=1, device_id={"dev": peers[mask]}, device_id_type=MESH
        )
    load_x = pltpu.make_async_copy(x_in, x_all.at[me], local_sem.at[0])
    load_w = pltpu.make_async_copy(w_in, w_own, local_sem.at[1])
    load_x.start()
    load_w.start()
    pl.semaphore_wait(barrier, images - 1)

    sends = []

    def send_half(mask, part, to, from_input=False):
        rows = pl.ds(part * half, half)
        source = x_in.at[rows] if from_input else x_all.at[peers[mask], rows]
        copy = pltpu.make_async_remote_copy(
            src_ref=source,
            dst_ref=x_all.at[peers[mask], rows],
            send_sem=x_send.at[len(sends)],
            recv_sem=x_recv.at[peers[mask], part],
            device_id={"dev": peers[to]},
            device_id_type=MESH,
        )
        copy.start()
        sends.append(copy)

    def await_half(mask, part):
        rows = pl.ds(part * half, half)
        pltpu.make_async_remote_copy(
            src_ref=x_all.at[peers[mask], rows],
            dst_ref=x_all.at[peers[mask], rows],
            send_sem=x_send.at[0],
            recv_sem=x_recv.at[peers[mask], part],
            device_id={"dev": peers[1]},
            device_id_type=MESH,
        ).wait_recv()

    send_half(0, 1, 2, True)
    send_half(0, 0, 4, True)
    send_half(0, 0, 2, True)
    send_half(0, 1, 4, True)
    send_half(0, 0, 1, True)
    send_half(0, 1, 1, True)

    per_group = 128 // own
    group = pl.multiple_of((me // per_group) * 128, 128)
    for row_tap in range(3):
        for col_tap in range(3):
            row = smooth_in[row_tap, pl.ds(col_tap, 1), pl.ds(group, 128)]
            smooth_wide[row_tap * 3 + col_tap] = jnp.broadcast_to(row, (128, 128)).T
    first = pl.multiple_of((me % per_group) * own, own)

    lane = lax.broadcasted_iota(jnp.int32, (1, positions), 1)
    keep_rows = [lane >= grid_cols, None, lane < positions - grid_cols]
    keep_cols = [lane % grid_cols > 0, None, lane % grid_cols < grid_cols - 1]

    def shift_row(values, tap):
        return values if tap == 1 else shift_lanes(values, (1 - tap) * grid_cols, keep_rows[tap])

    def shift_col(values, tap):
        return values if tap == 1 else shift_lanes(values, 1 - tap, keep_cols[tap])

    load_x.wait()
    load_w.wait()

    def convolve_pair(first_mask, second_mask):
        pair = (peers[first_mask], peers[second_mask])
        rows = jnp.concatenate([x_all[pair[0]], x_all[pair[1]]], axis=0)
        taps = lax.dot_general(
            w_own[...], rows, (((1,), (1,)), ((), ())), preferred_element_type=jnp.float32
        )
        for at in range(2):
            total = None
            for col_tap in range(3):
                column = None
                for row_tap in range(3):
                    tap = row_tap * 3 + col_tap
                    block = taps[tap * own : (tap + 1) * own, at * positions : (at + 1) * positions]
                    block = shift_row(block, row_tap)
                    column = block if column is None else column + block
                column = shift_col(column, col_tap)
                total = column if total is None else total + column
            feats[pair[at]] = total.astype(jnp.bfloat16).astype(jnp.float32)

    await_half(1, 0)
    await_half(1, 1)
    convolve_pair(0, 1)
    await_half(4, 0)
    send_half(4, 0, 2)
    await_half(2, 1)
    send_half(2, 1, 4)
    send_half(4, 0, 1)
    send_half(2, 1, 1)
    await_half(2, 0)
    send_half(2, 0, 1)
    await_half(4, 1)
    send_half(4, 1, 1)
    convolve_pair(2, 4)
    await_half(6, 0)
    send_half(6, 0, 1)
    await_half(6, 1)
    send_half(6, 1, 1)
    for mask in (3, 5):
        await_half(mask, 0)
        await_half(mask, 1)
    convolve_pair(3, 5)
    await_half(7, 0)
    await_half(7, 1)
    convolve_pair(6, 7)

    center = feats[0]
    for n in range(1, images):
        center = center + feats[n]
    center = center / images
    for n in range(images):
        feats[n] = (feats[n] - center).astype(jnp.bfloat16).astype(jnp.float32)
    for n in range(images):
        k_all[me, n] = jnp.sum(feats[n][None] * feats[...], axis=1)

    k_sends = []
    for mask in (6, 7, 2, 4, 3, 5, 1):
        copy = pltpu.make_async_remote_copy(
            src_ref=k_all.at[me],
            dst_ref=k_all.at[me],
            send_sem=k_send.at[mask],
            recv_sem=k_recv.at[me],
            device_id={"dev": peers[mask]},
            device_id_type=MESH,
        )
        copy.start()
        k_sends.append(copy)
    for mask in range(1, images):
        pltpu.make_async_remote_copy(
            src_ref=k_all.at[peers[mask]],
            dst_ref=k_all.at[peers[mask]],
            send_sem=k_send.at[mask],
            recv_sem=k_recv.at[peers[mask]],
            device_id={"dev": peers[mask]},
            device_id_type=MESH,
        ).wait_recv()

    shape = (images, images, positions)
    diagonal = lax.broadcasted_iota(jnp.int32, shape, 0) == lax.broadcasted_iota(
        jnp.int32, shape, 1
    )
    summed = k_all[0]
    for source in range(1, images):
        summed = summed + k_all[source]
    moments = summed / (images - 1) + jnp.where(diagonal, ridge_term, 0.0)
    squares = jnp.sum(jnp.sum(moments * moments, axis=0), axis=0, keepdims=True)
    frob = jnp.sqrt(squares + ridge_term * ridge_term * (channels - images))[None]
    upper = moments / frob
    lower = None
    for sweep in range(ITERS):
        product = upper if lower is None else small_product(lower, upper)
        factor = jnp.where(diagonal, 1.5, 0.0) - 0.5 * product
        if sweep + 1 < ITERS:
            upper = small_product(upper, factor)
        lower = factor if lower is None else small_product(factor, lower)
    mix[...] = lower / jnp.sqrt(frob)

    o_sends = []
    for mask in (6, 7, 2, 4, 3, 5, 1, 0):
        target = peers[mask]
        weights = mix[target]
        white = None
        for m in range(images):
            term = weights[m : m + 1, :] * feats[m]
            white = term if white is None else white + term
        white = white.astype(jnp.bfloat16).astype(jnp.float32)
        moved = [shift_col(white, col_tap) for col_tap in range(3)]
        smoothed = None
        for row_tap in range(3):
            line = None
            for col_tap in range(3):
                term = moved[col_tap] * smooth_wide[row_tap * 3 + col_tap, pl.ds(first, own)]
                line = term if line is None else line + term
            line = shift_row(line, row_tap)
            smoothed = line if smoothed is None else smoothed + line
        sent[mask] = smoothed.astype(jnp.bfloat16)
        if mask == 0:
            keep = pltpu.make_async_copy(sent.at[0], out_ref.at[me], local_sem.at[0])
            keep.start()
        else:
            copy = pltpu.make_async_remote_copy(
                src_ref=sent.at[mask],
                dst_ref=out_ref.at[me],
                send_sem=o_send.at[mask],
                recv_sem=o_recv.at[me],
                device_id={"dev": target},
                device_id_type=MESH,
            )
            copy.start()
            o_sends.append(copy)
    for copy in sends + k_sends:
        copy.wait_send()
    keep.wait()
    for mask in range(1, images):
        pltpu.make_async_remote_copy(
            src_ref=sent.at[mask],
            dst_ref=out_ref.at[peers[mask]],
            send_sem=o_send.at[mask],
            recv_sem=o_recv.at[peers[mask]],
            device_id={"dev": peers[mask]},
            device_id_type=MESH,
        ).wait_recv()
    for copy in o_sends:
        copy.wait_send()


def fused_shards(backbone, conv_weight, smooth_weight):
    _, grid_rows, grid_cols, channels = backbone.shape
    images = lax.axis_size("dev")
    positions = grid_rows * grid_cols
    own = conv_weight.shape[3]
    x = backbone.reshape(positions, channels)
    w = conv_weight.transpose(0, 1, 3, 2).reshape(9 * own, channels)
    any_space = pl.BlockSpec(memory_space=pl.ANY)
    vmem_space = pl.BlockSpec(memory_space=pltpu.VMEM)
    gathered = pl.pallas_call(
        functools.partial(fused_kernel, grid_cols, images, channels),
        out_shape=jax.ShapeDtypeStruct((images, own, positions), jnp.bfloat16),
        in_specs=[any_space, any_space, vmem_space],
        out_specs=any_space,
        scratch_shapes=[
            pltpu.VMEM((images, positions, channels), jnp.bfloat16),
            pltpu.VMEM((9 * own, channels), jnp.bfloat16),
            pltpu.VMEM((9, 128, 128), jnp.float32),
            pltpu.VMEM((images, own, positions), jnp.float32),
            pltpu.VMEM((images, images, images, positions), jnp.float32),
            pltpu.VMEM((images, images, positions), jnp.float32),
            pltpu.VMEM((images, own, positions), jnp.bfloat16),
            pltpu.SemaphoreType.DMA((2,)),
            pltpu.SemaphoreType.DMA((14,)),
            pltpu.SemaphoreType.DMA((images, 2)),
            pltpu.SemaphoreType.DMA((images,)),
            pltpu.SemaphoreType.DMA((images,)),
            pltpu.SemaphoreType.DMA((images,)),
            pltpu.SemaphoreType.DMA((images,)),
        ],
        compiler_params=pltpu.CompilerParams(
            collective_id=0, has_side_effects=True, vmem_limit_bytes=24 * 2**20
        ),
    )(x, w, smooth_weight)
    return gathered.reshape(channels, positions).T.reshape(backbone.shape)


def choose_shards(backbone, conv_weight, smooth_weight):
    local_images, grid_rows, grid_cols, _ = backbone.shape
    own = conv_weight.shape[3]
    fits = (
        local_images == 1
        and lax.axis_size("dev") == 2**3
        and grid_rows * grid_cols == 128
        and own % 16 == 0
        and 128 % own == 0
    )
    form = fused_shards if fits else shards
    return form(backbone, conv_weight, smooth_weight)


def solution(mesh):
    placed = (
        P(("rep", "dev"), None, None, None),
        P(None, None, None, ("rep", "dev")),
        P(None, None, "rep"),
    )
    return jax.shard_map(
        choose_shards,
        mesh=mesh,
        in_specs=placed,
        out_specs=P(("rep", "dev"), None, None, None),
        check_vma=False,
    )
```

```python
import functools

import jax
import jax.numpy as jnp
from jax import lax
from jax.experimental import pallas as pl
from jax.experimental.pallas import tpu as pltpu
from jax.sharding import PartitionSpec as P

ITERS = 2
MESH = pl.DeviceIdType.MESH
PIECES = 2


ridge_term = 0.5


def convolve(padded, weights, grid_rows, grid_cols):
    summed = None
    for row_tap in range(3):
        for col_tap in range(3):
            window = padded[:, row_tap : row_tap + grid_rows, col_tap : col_tap + grid_cols, :]
            flat_window = window.reshape(-1, window.shape[3])
            product = jnp.dot(
                flat_window, weights[row_tap, col_tap], preferred_element_type=jnp.float32
            )
            summed = product if summed is None else summed + product
    return summed.reshape(padded.shape[0], grid_rows, grid_cols, weights.shape[3])


def single_root(moments):
    identity = jnp.eye(moments.shape[0], dtype=jnp.float32)
    frob = jnp.sqrt(jnp.sum(moments * moments))
    upper = moments / frob
    lower = identity
    for sweep in range(ITERS):
        product = jnp.dot(lower, upper, precision=lax.Precision.HIGHEST)
        factor = 1.5 * identity - 0.5 * product
        if sweep + 1 < ITERS:
            upper = jnp.dot(upper, factor, precision=lax.Precision.HIGHEST)
        lower = jnp.dot(factor, lower, precision=lax.Precision.HIGHEST)
    return lower / jnp.sqrt(frob)


def whiten_block(received):
    features_block = received[:, 0]
    image_count = features_block.shape[0]
    channels = features_block.shape[2]
    identity = jnp.eye(channels, dtype=jnp.float32)
    center = jnp.sum(features_block.astype(jnp.float32), axis=0) / image_count
    centered = (features_block.astype(jnp.float32) - center).astype(jnp.bfloat16)
    gram = jnp.einsum("nkc,nkd->kcd", centered, centered, preferred_element_type=jnp.float32)
    moments = gram / (image_count - 1) + ridge_term * identity
    roots = lax.map(single_root, moments)
    roots = roots.astype(jnp.bfloat16)
    whitened = jnp.einsum(
        "nkc,kcd->nkd", centered, roots, preferred_element_type=jnp.float32
    ).astype(jnp.bfloat16)
    return whitened[:, None]


def shards(backbone, conv_weight, smooth_weight):
    local_images = backbone.shape[0]
    grid_rows = backbone.shape[1]
    grid_cols = backbone.shape[2]
    channels = backbone.shape[3]
    owners = lax.axis_size("dev")
    padded = jnp.pad(backbone, ((0, 0), (1, 1), (1, 1), (0, 0)))
    kernel = lax.all_gather(conv_weight, "dev", axis=3, tiled=True)
    conv_out = convolve(padded, kernel, grid_rows, grid_cols)
    per_owner = grid_rows * grid_cols // owners
    features = conv_out.astype(jnp.bfloat16).reshape(local_images, owners, per_owner, channels)
    whitened = whiten_block(
        lax.all_to_all(features, "dev", split_axis=1, concat_axis=0, tiled=True)
    )
    returned = lax.all_to_all(whitened, "dev", split_axis=0, concat_axis=1, tiled=True)
    returned = returned.reshape(local_images, grid_rows, grid_cols, channels)
    padded_white = jnp.pad(returned, ((0, 0), (1, 1), (1, 1), (0, 0)))
    summed = jnp.zeros((local_images, grid_rows, grid_cols, channels), jnp.float32)
    for row_tap in range(3):
        for col_tap in range(3):
            window = padded_white[
                :, row_tap : row_tap + grid_rows, col_tap : col_tap + grid_cols, :
            ]
            summed = summed + window.astype(jnp.float32) * smooth_weight[row_tap, col_tap]
    return summed.astype(jnp.bfloat16)


def flip(index, mask, bits):
    flipped = 0
    for bit in range(bits):
        digit = (index // 2**bit) % 2
        if (mask >> bit) & 1:
            digit = 1 - digit
        flipped = flipped + digit * 2**bit
    return flipped


def shift_lanes(values, step, keep):
    lanes = values.shape[-1]
    return jnp.where(keep, pltpu.roll(values, step % lanes, values.ndim - 1), 0.0)


def fused_kernel(
    grid_cols,
    images,
    channels,
    x_in,
    w_in,
    smooth_in,
    out_ref,
    x_all,
    w_own,
    smooth_own,
    smooth_wide,
    feats,
    k_all,
    mix,
    sent,
    local_sem,
    x_send,
    x_recv,
    k_send,
    k_recv,
    o_send,
    o_recv,
):
    bits = 3
    me = lax.axis_index("dev")
    positions = x_in.shape[0]
    own = feats.shape[1]
    piece = positions // PIECES
    peers = [flip(me, mask, bits) for mask in range(images)]

    barrier = pltpu.get_barrier_semaphore()
    for mask in range(1, images):
        pl.semaphore_signal(
            barrier, inc=1, device_id={"dev": peers[mask]}, device_id_type=MESH
        )
    load_x = pltpu.make_async_copy(x_in, x_all.at[me], local_sem.at[0])
    load_w = pltpu.make_async_copy(w_in, w_own, local_sem.at[1])
    load_smooth = pltpu.make_async_copy(smooth_in, smooth_own, local_sem.at[2])
    load_x.start()
    load_w.start()
    load_smooth.start()
    pl.semaphore_wait(barrier, images - 1)

    sends = []

    def send_piece(mask, part, to, from_input=False):
        rows = pl.ds(part * piece, piece)
        source = x_in.at[rows] if from_input else x_all.at[peers[mask], rows]
        copy = pltpu.make_async_remote_copy(
            src_ref=source,
            dst_ref=x_all.at[peers[mask], rows],
            send_sem=x_send.at[len(sends)],
            recv_sem=x_recv.at[peers[mask], part],
            device_id={"dev": peers[to]},
            device_id_type=MESH,
        )
        copy.start()
        sends.append(copy)

    def await_piece(mask, part):
        rows = pl.ds(part * piece, piece)
        pltpu.make_async_remote_copy(
            src_ref=x_all.at[peers[mask], rows],
            dst_ref=x_all.at[peers[mask], rows],
            send_sem=x_send.at[0],
            recv_sem=x_recv.at[peers[mask], part],
            device_id={"dev": peers[1]},
            device_id_type=MESH,
        ).wait_recv()

    by_x = range(PIECES // 2)
    by_y = range(PIECES // 2, PIECES)
    for part in range(PIECES):
        send_piece(0, part, 1, True)
    for low, high in zip(by_x, by_y):
        send_piece(0, high, 2, True)
        send_piece(0, low, 4, True)
    for copy in sends[PIECES:]:
        copy.wait_send()
    to_wait = sends[:PIECES]
    already = len(sends)
    for low, high in zip(by_x, by_y):
        send_piece(0, low, 2, True)
        send_piece(0, high, 4, True)

    load_smooth.wait()
    per_group = 128 // own
    group = pl.multiple_of((me // per_group) * 128, 128)
    for row_tap in range(3):
        for col_tap in range(3):
            row = smooth_own[row_tap, pl.ds(col_tap, 1), pl.ds(group, 128)]
            smooth_wide[row_tap * 3 + col_tap] = jnp.broadcast_to(row, (128, 128)).T
    first = pl.multiple_of((me % per_group) * own, own)

    lane = lax.broadcasted_iota(jnp.int32, (1, positions), 1)
    keep_rows = [lane >= grid_cols, None, lane < positions - grid_cols]
    keep_cols = [lane % grid_cols > 0, None, lane % grid_cols < grid_cols - 1]

    def shift_row(values, tap):
        return values if tap == 1 else shift_lanes(values, (1 - tap) * grid_cols, keep_rows[tap])

    def shift_col(values, tap):
        return values if tap == 1 else shift_lanes(values, 1 - tap, keep_cols[tap])

    load_x.wait()
    load_w.wait()

    def convolve_pair(first_mask, second_mask):
        pair = (peers[first_mask], peers[second_mask])
        rows = jnp.concatenate([x_all[pair[0]], x_all[pair[1]]], axis=0)
        taps = lax.dot_general(
            w_own[...], rows, (((1,), (1,)), ((), ())), preferred_element_type=jnp.float32
        )
        for at in range(2):
            total = None
            for col_tap in range(3):
                column = None
                for row_tap in range(3):
                    tap = row_tap * 3 + col_tap
                    block = taps[tap * own : (tap + 1) * own, at * positions : (at + 1) * positions]
                    block = shift_row(block, row_tap)
                    column = block if column is None else column + block
                column = shift_col(column, col_tap)
                total = column if total is None else total + column
            feats[pair[at]] = total.astype(jnp.bfloat16).astype(jnp.float32)

    for part in range(PIECES):
        await_piece(1, part)
    convolve_pair(0, 1)
    for low, high in zip(by_x, by_y):
        await_piece(4, low)
        send_piece(4, low, 2)
        await_piece(2, high)
        send_piece(2, high, 4)
        send_piece(4, low, 1)
        send_piece(2, high, 1)
    for low, high in zip(by_x, by_y):
        await_piece(2, low)
        send_piece(2, low, 1)
        await_piece(4, high)
        send_piece(4, high, 1)
    convolve_pair(2, 4)
    for low, high in zip(by_x, by_y):
        await_piece(6, low)
        send_piece(6, low, 1)
        await_piece(6, high)
        send_piece(6, high, 1)
    for mask in (3, 5):
        for part in range(PIECES):
            await_piece(mask, part)
    convolve_pair(3, 5)
    for part in range(PIECES):
        await_piece(7, part)
    convolve_pair(6, 7)

    center = feats[0]
    for n in range(1, images):
        center = center + feats[n]
    center = center / images
    for n in range(images):
        feats[n] = (feats[n] - center).astype(jnp.bfloat16).astype(jnp.float32)
    stored = images // 2 + 1
    values = feats[...]
    diagonals = []
    for k in range(stored):
        turned = values if k == 0 else jnp.concatenate([values[k:], values[:k]], axis=0)
        diagonals.append(jnp.sum(values * turned, axis=1))
    spare = k_all.shape[1] - stored * images
    if spare:
        diagonals.append(jnp.zeros((spare, positions), jnp.float32))
    k_all[me] = jnp.concatenate(diagonals, axis=0).astype(k_all.dtype)

    k_sends = []
    for mask in (6, 7, 2, 4, 3, 5, 1):
        copy = pltpu.make_async_remote_copy(
            src_ref=k_all.at[me],
            dst_ref=k_all.at[me],
            send_sem=k_send.at[mask],
            recv_sem=k_recv.at[me],
            device_id={"dev": peers[mask]},
            device_id_type=MESH,
        )
        copy.start()
        k_sends.append(copy)
    for mask in range(1, images):
        pltpu.make_async_remote_copy(
            src_ref=k_all.at[peers[mask]],
            dst_ref=k_all.at[peers[mask]],
            send_sem=k_send.at[mask],
            recv_sem=k_recv.at[peers[mask]],
            device_id={"dev": peers[mask]},
            device_id_type=MESH,
        ).wait_recv()

    summed = k_all[0].astype(jnp.float32)
    for source in range(1, images):
        summed = summed + k_all[source].astype(jnp.float32)

    def complete(half):
        return half + [pltpu.roll(half[images - k], images - k, 0) for k in range(stored, images)]

    def product_of(left, right):
        full_left, full_right = complete(left), complete(right)
        result = []
        for k in range(stored):
            entry = None
            for j in range(images):
                other = full_right[(k - j) % images]
                if j:
                    other = pltpu.roll(other, images - j, 0)
                term = full_left[j] * other
                entry = term if entry is None else entry + term
            result.append(entry)
        return result

    moments = [summed[k * images : (k + 1) * images] / (images - 1) for k in range(stored)]
    moments[0] = moments[0] + ridge_term
    squares = sum(entry * entry for entry in complete(moments))
    squares = jnp.sum(squares, axis=0, keepdims=True)
    frob = jnp.sqrt(squares + ridge_term * ridge_term * (channels - images))
    upper = [entry / frob for entry in moments]
    lower = None
    for sweep in range(ITERS):
        product = upper if lower is None else product_of(lower, upper)
        factor = [-0.5 * entry for entry in product]
        factor[0] = factor[0] + 1.5
        if sweep + 1 < ITERS:
            upper = product_of(upper, factor)
        lower = factor if lower is None else product_of(factor, lower)
    for k, entry in enumerate(complete(lower)):
        mix[k] = entry / jnp.sqrt(frob)

    o_sends = []
    for mask in (6, 7, 2, 4, 3, 5, 1, 0):
        target = peers[mask]
        white = None
        for k in range(images):
            term = mix[k, pl.ds(target, 1)] * feats[(target + k) % images]
            white = term if white is None else white + term
        white = white.astype(jnp.bfloat16).astype(jnp.float32)
        moved = [shift_col(white, col_tap) for col_tap in range(3)]
        smoothed = None
        for row_tap in range(3):
            line = None
            for col_tap in range(3):
                term = moved[col_tap] * smooth_wide[row_tap * 3 + col_tap, pl.ds(first, own)]
                line = term if line is None else line + term
            line = shift_row(line, row_tap)
            smoothed = line if smoothed is None else smoothed + line
        sent[mask] = smoothed.astype(jnp.bfloat16)
        if mask == 0:
            keep = pltpu.make_async_copy(sent.at[0], out_ref.at[me], local_sem.at[0])
            keep.start()
        else:
            copy = pltpu.make_async_remote_copy(
                src_ref=sent.at[mask],
                dst_ref=out_ref.at[me],
                send_sem=o_send.at[mask],
                recv_sem=o_recv.at[me],
                device_id={"dev": target},
                device_id_type=MESH,
            )
            copy.start()
            o_sends.append(copy)
    for copy in to_wait + sends[already:] + k_sends:
        copy.wait_send()
    keep.wait()
    for mask in range(1, images):
        pltpu.make_async_remote_copy(
            src_ref=sent.at[mask],
            dst_ref=out_ref.at[peers[mask]],
            send_sem=o_send.at[mask],
            recv_sem=o_recv.at[peers[mask]],
            device_id={"dev": peers[mask]},
            device_id_type=MESH,
        ).wait_recv()
    for copy in o_sends:
        copy.wait_send()


def fused_shards(backbone, conv_weight, smooth_weight):
    _, grid_rows, grid_cols, channels = backbone.shape
    images = lax.axis_size("dev")
    positions = grid_rows * grid_cols
    own = conv_weight.shape[3]
    x = backbone.reshape(positions, channels)
    w = conv_weight.transpose(0, 1, 3, 2).reshape(9 * own, channels)
    hbm_space = pl.BlockSpec(memory_space=pltpu.HBM)
    packed = pl.cdiv((images // 2 + 1) * images, 16) * 16
    gathered = pl.pallas_call(
        functools.partial(fused_kernel, grid_cols, images, channels),
        out_shape=jax.ShapeDtypeStruct((images, own, positions), jnp.bfloat16),
        in_specs=[hbm_space] * 3,
        out_specs=hbm_space,
        scratch_shapes=[
            pltpu.VMEM((images, positions, channels), jnp.bfloat16),
            pltpu.VMEM((9 * own, channels), jnp.bfloat16),
            pltpu.VMEM(smooth_weight.shape, jnp.float32),
            pltpu.VMEM((9, 128, 128), jnp.float32),
            pltpu.VMEM((images, own, positions), jnp.float32),
            pltpu.VMEM((images, packed, positions), jnp.bfloat16),
            pltpu.VMEM((images, images, positions), jnp.float32),
            pltpu.VMEM((images, own, positions), jnp.bfloat16),
            pltpu.SemaphoreType.DMA((3,)),
            pltpu.SemaphoreType.DMA((7 * PIECES,)),
            pltpu.SemaphoreType.DMA((images, PIECES)),
            pltpu.SemaphoreType.DMA((images,)),
            pltpu.SemaphoreType.DMA((images,)),
            pltpu.SemaphoreType.DMA((images,)),
            pltpu.SemaphoreType.DMA((images,)),
        ],
        compiler_params=pltpu.CompilerParams(
            collective_id=0, has_side_effects=True, vmem_limit_bytes=60 * 2**20
        ),
    )(x, w, smooth_weight)
    return gathered.reshape(channels, positions).T.reshape(backbone.shape)


def choose_shards(backbone, conv_weight, smooth_weight):
    local_images, grid_rows, grid_cols, _ = backbone.shape
    own = conv_weight.shape[3]
    fits = (
        local_images == 1
        and lax.axis_size("dev") == 2**3
        and grid_rows * grid_cols == 128
        and own % 16 == 0
        and 128 % own == 0
    )
    form = fused_shards if fits else shards
    return form(backbone, conv_weight, smooth_weight)


def solution(mesh):
    placed = (
        P(("rep", "dev"), None, None, None),
        P(None, None, None, ("rep", "dev")),
        P(None, None, "rep"),
    )
    return jax.shard_map(
        choose_shards,
        mesh=mesh,
        in_specs=placed,
        out_specs=P(("rep", "dev"), None, None, None),
        check_vma=False,
    )
```

```python
import functools

import jax
import jax.numpy as jnp
from jax import lax
from jax.experimental import pallas as pl
from jax.experimental.pallas import tpu as pltpu
from jax.sharding import PartitionSpec as P

ITERS = 2
MESH = pl.DeviceIdType.MESH
PIECES = 2


ridge_term = 0.5


def convolve(padded, weights, grid_rows, grid_cols):
    summed = None
    for row_tap in range(3):
        for col_tap in range(3):
            window = padded[:, row_tap : row_tap + grid_rows, col_tap : col_tap + grid_cols, :]
            flat_window = window.reshape(-1, window.shape[3])
            product = jnp.dot(
                flat_window, weights[row_tap, col_tap], preferred_element_type=jnp.float32
            )
            summed = product if summed is None else summed + product
    return summed.reshape(padded.shape[0], grid_rows, grid_cols, weights.shape[3])


def single_root(moments):
    identity = jnp.eye(moments.shape[0], dtype=jnp.float32)
    frob = jnp.sqrt(jnp.sum(moments * moments))
    upper = moments / frob
    lower = identity
    for sweep in range(ITERS):
        product = jnp.dot(lower, upper, precision=lax.Precision.HIGHEST)
        factor = 1.5 * identity - 0.5 * product
        if sweep + 1 < ITERS:
            upper = jnp.dot(upper, factor, precision=lax.Precision.HIGHEST)
        lower = jnp.dot(factor, lower, precision=lax.Precision.HIGHEST)
    return lower / jnp.sqrt(frob)


def whiten_block(received):
    features_block = received[:, 0]
    image_count = features_block.shape[0]
    channels = features_block.shape[2]
    identity = jnp.eye(channels, dtype=jnp.float32)
    center = jnp.sum(features_block.astype(jnp.float32), axis=0) / image_count
    centered = (features_block.astype(jnp.float32) - center).astype(jnp.bfloat16)
    gram = jnp.einsum("nkc,nkd->kcd", centered, centered, preferred_element_type=jnp.float32)
    moments = gram / (image_count - 1) + ridge_term * identity
    roots = lax.map(single_root, moments)
    roots = roots.astype(jnp.bfloat16)
    whitened = jnp.einsum(
        "nkc,kcd->nkd", centered, roots, preferred_element_type=jnp.float32
    ).astype(jnp.bfloat16)
    return whitened[:, None]


def shards(backbone, conv_weight, smooth_weight):
    local_images = backbone.shape[0]
    grid_rows = backbone.shape[1]
    grid_cols = backbone.shape[2]
    channels = backbone.shape[3]
    owners = lax.axis_size("dev")
    padded = jnp.pad(backbone, ((0, 0), (1, 1), (1, 1), (0, 0)))
    kernel = lax.all_gather(conv_weight, "dev", axis=3, tiled=True)
    conv_out = convolve(padded, kernel, grid_rows, grid_cols)
    per_owner = grid_rows * grid_cols // owners
    features = conv_out.astype(jnp.bfloat16).reshape(local_images, owners, per_owner, channels)
    whitened = whiten_block(
        lax.all_to_all(features, "dev", split_axis=1, concat_axis=0, tiled=True)
    )
    returned = lax.all_to_all(whitened, "dev", split_axis=0, concat_axis=1, tiled=True)
    returned = returned.reshape(local_images, grid_rows, grid_cols, channels)
    padded_white = jnp.pad(returned, ((0, 0), (1, 1), (1, 1), (0, 0)))
    summed = jnp.zeros((local_images, grid_rows, grid_cols, channels), jnp.float32)
    for row_tap in range(3):
        for col_tap in range(3):
            window = padded_white[
                :, row_tap : row_tap + grid_rows, col_tap : col_tap + grid_cols, :
            ]
            summed = summed + window.astype(jnp.float32) * smooth_weight[row_tap, col_tap]
    return summed.astype(jnp.bfloat16)


def flip(index, mask, bits):
    flipped = 0
    for bit in range(bits):
        digit = (index // 2**bit) % 2
        if (mask >> bit) & 1:
            digit = 1 - digit
        flipped = flipped + digit * 2**bit
    return flipped


def shift_lanes(values, step, keep):
    lanes = values.shape[-1]
    return jnp.where(keep, pltpu.roll(values, step % lanes, values.ndim - 1), 0.0)


def fused_kernel(
    grid_cols,
    images,
    channels,
    x_in,
    w_in,
    smooth_in,
    out_ref,
    x_all,
    w_own,
    smooth_own,
    smooth_wide,
    feats,
    k_all,
    mix,
    sent,
    local_sem,
    x_send,
    x_recv,
    k_send,
    k_recv,
    o_send,
    o_recv,
):
    bits = 3
    me = lax.axis_index("dev")
    positions = x_in.shape[0]
    own = feats.shape[1]
    piece = positions // PIECES
    peers = [flip(me, mask, bits) for mask in range(images)]

    barrier = pltpu.get_barrier_semaphore()
    for mask in range(1, images):
        pl.semaphore_signal(
            barrier, inc=1, device_id={"dev": peers[mask]}, device_id_type=MESH
        )
    load_x = pltpu.make_async_copy(x_in, x_all.at[me], local_sem.at[0])
    load_w = pltpu.make_async_copy(w_in, w_own, local_sem.at[1])
    load_smooth = pltpu.make_async_copy(smooth_in, smooth_own, local_sem.at[2])
    load_x.start()
    load_w.start()
    load_smooth.start()
    pl.semaphore_wait(barrier, images - 1)

    sends = []

    def send_piece(mask, part, to, from_input=False):
        rows = pl.ds(part * piece, piece)
        source = x_in.at[rows] if from_input else x_all.at[peers[mask], rows]
        copy = pltpu.make_async_remote_copy(
            src_ref=source,
            dst_ref=x_all.at[peers[mask], rows],
            send_sem=x_send.at[len(sends)],
            recv_sem=x_recv.at[peers[mask], part],
            device_id={"dev": peers[to]},
            device_id_type=MESH,
        )
        copy.start()
        sends.append(copy)

    def await_piece(mask, part):
        rows = pl.ds(part * piece, piece)
        pltpu.make_async_remote_copy(
            src_ref=x_all.at[peers[mask], rows],
            dst_ref=x_all.at[peers[mask], rows],
            send_sem=x_send.at[0],
            recv_sem=x_recv.at[peers[mask], part],
            device_id={"dev": peers[1]},
            device_id_type=MESH,
        ).wait_recv()

    by_x = range(PIECES // 2)
    by_y = range(PIECES // 2, PIECES)
    for part in range(PIECES):
        send_piece(0, part, 1, True)
    for low, high in zip(by_x, by_y):
        send_piece(0, high, 2, True)
        send_piece(0, low, 4, True)
    for copy in sends[PIECES:]:
        copy.wait_send()
    to_wait = sends[:PIECES]
    already = len(sends)
    for low, high in zip(by_x, by_y):
        send_piece(0, low, 2, True)
        send_piece(0, high, 4, True)

    load_smooth.wait()
    per_group = 128 // own
    group = pl.multiple_of((me // per_group) * 128, 128)
    for row_tap in range(3):
        for col_tap in range(3):
            row = smooth_own[row_tap, pl.ds(col_tap, 1), pl.ds(group, 128)]
            smooth_wide[row_tap * 3 + col_tap] = jnp.broadcast_to(row, (128, 128)).T
    first = pl.multiple_of((me % per_group) * own, own)

    lane = lax.broadcasted_iota(jnp.int32, (1, positions), 1)
    keep_rows = [lane >= grid_cols, None, lane < positions - grid_cols]
    keep_cols = [lane % grid_cols > 0, None, lane % grid_cols < grid_cols - 1]

    def shift_row(values, tap):
        return values if tap == 1 else shift_lanes(values, (1 - tap) * grid_cols, keep_rows[tap])

    def shift_col(values, tap):
        return values if tap == 1 else shift_lanes(values, 1 - tap, keep_cols[tap])

    load_x.wait()
    load_w.wait()

    def convolve_group(*masks):
        group = [peers[mask] for mask in masks]
        rows = jnp.concatenate([x_all[at] for at in group], axis=0)
        taps = lax.dot_general(
            w_own[...], rows, (((1,), (1,)), ((), ())), preferred_element_type=jnp.float32
        )
        for at in range(len(group)):
            total = None
            for col_tap in range(3):
                column = None
                for row_tap in range(3):
                    tap = row_tap * 3 + col_tap
                    block = taps[tap * own : (tap + 1) * own, at * positions : (at + 1) * positions]
                    block = shift_row(block, row_tap)
                    column = block if column is None else column + block
                column = shift_col(column, col_tap)
                total = column if total is None else total + column
            feats[group[at]] = total.astype(jnp.bfloat16).astype(jnp.float32)

    for part in range(PIECES):
        await_piece(1, part)
    convolve_group(0, 1)
    for low, high in zip(by_x, by_y):
        await_piece(4, low)
        send_piece(4, low, 2)
        await_piece(2, high)
        send_piece(2, high, 4)
        send_piece(4, low, 1)
        send_piece(2, high, 1)
    for low, high in zip(by_x, by_y):
        await_piece(2, low)
        send_piece(2, low, 1)
        await_piece(4, high)
        send_piece(4, high, 1)
    convolve_group(2, 4)
    for low, high in zip(by_x, by_y):
        await_piece(6, low)
        send_piece(6, low, 1)
        await_piece(6, high)
        send_piece(6, high, 1)
    for mask in (3, 5):
        for part in range(PIECES):
            await_piece(mask, part)
    convolve_group(3, 5, 6)
    for part in range(PIECES):
        await_piece(7, part)
    convolve_group(7)

    center = feats[0]
    for n in range(1, images):
        center = center + feats[n]
    center = center / images
    for n in range(images):
        feats[n] = (feats[n] - center).astype(jnp.bfloat16).astype(jnp.float32)
    stored = images // 2 + 1
    values = feats[...]
    diagonals = []
    for k in range(stored):
        turned = values if k == 0 else jnp.concatenate([values[k:], values[:k]], axis=0)
        diagonals.append(jnp.sum(values * turned, axis=1))
    spare = k_all.shape[1] - stored * images
    if spare:
        diagonals.append(jnp.zeros((spare, positions), jnp.float32))
    k_all[me] = jnp.concatenate(diagonals, axis=0).astype(k_all.dtype)

    k_sends = []
    for mask in (6, 7, 2, 4, 3, 5, 1):
        copy = pltpu.make_async_remote_copy(
            src_ref=k_all.at[me],
            dst_ref=k_all.at[me],
            send_sem=k_send.at[mask],
            recv_sem=k_recv.at[me],
            device_id={"dev": peers[mask]},
            device_id_type=MESH,
        )
        copy.start()
        k_sends.append(copy)
    for mask in range(1, images):
        pltpu.make_async_remote_copy(
            src_ref=k_all.at[peers[mask]],
            dst_ref=k_all.at[peers[mask]],
            send_sem=k_send.at[mask],
            recv_sem=k_recv.at[peers[mask]],
            device_id={"dev": peers[mask]},
            device_id_type=MESH,
        ).wait_recv()

    summed = k_all[0].astype(jnp.float32)
    for source in range(1, images):
        summed = summed + k_all[source].astype(jnp.float32)

    def complete(half):
        return half + [pltpu.roll(half[images - k], images - k, 0) for k in range(stored, images)]

    def product_of(left, right):
        full_left, full_right = complete(left), complete(right)
        result = []
        for k in range(stored):
            entry = None
            for j in range(images):
                other = full_right[(k - j) % images]
                if j:
                    other = pltpu.roll(other, images - j, 0)
                term = full_left[j] * other
                entry = term if entry is None else entry + term
            result.append(entry)
        return result

    moments = [summed[k * images : (k + 1) * images] / (images - 1) for k in range(stored)]
    moments[0] = moments[0] + ridge_term
    squares = sum(entry * entry for entry in complete(moments))
    squares = jnp.sum(squares, axis=0, keepdims=True)
    frob = jnp.sqrt(squares + ridge_term * ridge_term * (channels - images))
    upper = [entry / frob for entry in moments]
    lower = None
    for sweep in range(ITERS):
        product = upper if lower is None else product_of(lower, upper)
        factor = [-0.5 * entry for entry in product]
        factor[0] = factor[0] + 1.5
        if sweep + 1 < ITERS:
            upper = product_of(upper, factor)
        lower = factor if lower is None else product_of(factor, lower)
    for k, entry in enumerate(complete(lower)):
        mix[k] = entry / jnp.sqrt(frob)

    o_sends = []
    for mask in (6, 7, 2, 4, 3, 5, 1, 0):
        target = peers[mask]
        white = None
        for k in range(images):
            term = mix[k, pl.ds(target, 1)] * feats[(target + k) % images]
            white = term if white is None else white + term
        white = white.astype(jnp.bfloat16).astype(jnp.float32)
        moved = [shift_col(white, col_tap) for col_tap in range(3)]
        smoothed = None
        for row_tap in range(3):
            line = None
            for col_tap in range(3):
                term = moved[col_tap] * smooth_wide[row_tap * 3 + col_tap, pl.ds(first, own)]
                line = term if line is None else line + term
            line = shift_row(line, row_tap)
            smoothed = line if smoothed is None else smoothed + line
        sent[mask] = smoothed.astype(jnp.bfloat16)
        if mask == 0:
            keep = pltpu.make_async_copy(sent.at[0], out_ref.at[me], local_sem.at[0])
            keep.start()
        else:
            copy = pltpu.make_async_remote_copy(
                src_ref=sent.at[mask],
                dst_ref=out_ref.at[me],
                send_sem=o_send.at[mask],
                recv_sem=o_recv.at[me],
                device_id={"dev": target},
                device_id_type=MESH,
            )
            copy.start()
            o_sends.append(copy)
    for copy in to_wait + sends[already:] + k_sends:
        copy.wait_send()
    keep.wait()
    for mask in range(1, images):
        pltpu.make_async_remote_copy(
            src_ref=sent.at[mask],
            dst_ref=out_ref.at[peers[mask]],
            send_sem=o_send.at[mask],
            recv_sem=o_recv.at[peers[mask]],
            device_id={"dev": peers[mask]},
            device_id_type=MESH,
        ).wait_recv()
    for copy in o_sends:
        copy.wait_send()


def fused_shards(backbone, conv_weight, smooth_weight):
    _, grid_rows, grid_cols, channels = backbone.shape
    images = lax.axis_size("dev")
    positions = grid_rows * grid_cols
    own = conv_weight.shape[3]
    x = backbone.reshape(positions, channels)
    w = conv_weight.transpose(0, 1, 3, 2).reshape(9 * own, channels)
    hbm_space = pl.BlockSpec(memory_space=pltpu.HBM)
    packed = pl.cdiv((images // 2 + 1) * images, 16) * 16
    gathered = pl.pallas_call(
        functools.partial(fused_kernel, grid_cols, images, channels),
        out_shape=jax.ShapeDtypeStruct((images, own, positions), jnp.bfloat16),
        in_specs=[hbm_space] * 3,
        out_specs=hbm_space,
        scratch_shapes=[
            pltpu.VMEM((images, positions, channels), jnp.bfloat16),
            pltpu.VMEM((9 * own, channels), jnp.bfloat16),
            pltpu.VMEM(smooth_weight.shape, jnp.float32),
            pltpu.VMEM((9, 128, 128), jnp.float32),
            pltpu.VMEM((images, own, positions), jnp.float32),
            pltpu.VMEM((images, packed, positions), jnp.bfloat16),
            pltpu.VMEM((images, images, positions), jnp.float32),
            pltpu.VMEM((images, own, positions), jnp.bfloat16),
            pltpu.SemaphoreType.DMA((3,)),
            pltpu.SemaphoreType.DMA((7 * PIECES,)),
            pltpu.SemaphoreType.DMA((images, PIECES)),
            pltpu.SemaphoreType.DMA((images,)),
            pltpu.SemaphoreType.DMA((images,)),
            pltpu.SemaphoreType.DMA((images,)),
            pltpu.SemaphoreType.DMA((images,)),
        ],
        compiler_params=pltpu.CompilerParams(
            collective_id=0, has_side_effects=True, vmem_limit_bytes=60 * 2**20
        ),
    )(x, w, smooth_weight)
    return gathered.reshape(channels, positions).T.reshape(backbone.shape)


def choose_shards(backbone, conv_weight, smooth_weight):
    local_images, grid_rows, grid_cols, _ = backbone.shape
    own = conv_weight.shape[3]
    fits = (
        local_images == 1
        and lax.axis_size("dev") == 2**3
        and grid_rows * grid_cols == 128
        and own % 16 == 0
        and 128 % own == 0
    )
    form = fused_shards if fits else shards
    return form(backbone, conv_weight, smooth_weight)


def solution(mesh):
    placed = (
        P(("rep", "dev"), None, None, None),
        P(None, None, None, ("rep", "dev")),
        P(None, None, "rep"),
    )
    return jax.shard_map(
        choose_shards,
        mesh=mesh,
        in_specs=placed,
        out_specs=P(("rep", "dev"), None, None, None),
        check_vma=False,
    )
```
